256 devices in a mesh: region: 8 (over x, core), box: 32 (over y, z).
Axes of the slice: x: 4, y: 4, z: 8, core: 2. Of those that a mesh axis runs over, the one named last changes fastest.
Arguments:
- kept_diagonal_tile: bfloat16 [512, 512, 512], P(('region', 'box')), may hold values from -6 to 6
- discard_reciprocal: bfloat16 [512, 512, 512], P(('region', 'box')), may hold values from -0.25 to 0.25
- discard_by_kept: bfloat16 [512, 512, 512], P(('region', 'box')), may hold values from -6 to 6
- kept_by_discard: bfloat16 [512, 512, 512], P(('region', 'box')), may hold values from -0.25 to 0.25
- adjacent_discard_to_kept: bfloat16 [512, 4, 512, 512], P(('region', 'box')), may hold values from -0.25 to 0.25
- adjacent_kept_to_discard: bfloat16 [512, 4, 512, 512], P(('region', 'box')), may hold values from -6 to 6
- adjacent_site_table: int32 [512, 4], P(('region', 'box')), may hold values from 0 to 2
- retained_slots: int32 [512, 256], P(('region', 'box')), may hold values from 0 to 511, as said below
- kept_list_length: int32 [512], P(('region', 'box')), may hold values from 128 to 256, as said below
- ancestor_site_map: int32 [512], P(('region', 'box')), may hold values from 0 to 15, as said below
Outputs:
- parent_blocks: bfloat16 [512, 256, 256], P(('region', 'box'))
The draws below stay inside these ranges and needn't reach their ends.
Inputs may be any that keep to these rules, and one draw needn't show every extreme that they name: `retained_slots`: each row holds 256 different tile positions. `kept_list_length`: some box has all 256 entries valid. `ancestor_site_map`: among the boxes of one position j, every value from 0 to 15 occurs exactly once. `adjacent_site_table`: the value 2 marks an absent neighbour.
All inputs are finite; a program needn't handle non-finite values.
Results may differ from the reference program's by a relative error of at most 0.0053.
Values may be sent and summed in bfloat16 or wider, within the bound.
No kernel may reach another device: no remote copies, remote signals or barrier semaphores. Data moves between devices by JAX's collectives and lax.ppermute only.
A program may use at most 128 MiB of HBM per device.

```python
import jax
import jax.numpy as jnp
from jax import lax

S = 512
R = 512
SK = 256
NEAR = 4
BOX_DEV = 2
REGIONS = 8
COLUMNS = 32
BOXES = 512


def draw_retained_slots(key, part):
    key = jax.random.fold_in(key, 11)
    scores = jax.random.randint(key, (BOXES, S), 0, 1 << 20) * S + jnp.arange(S, dtype=jnp.int32)[None, :]
    picked_values = lax.top_k(scores, SK)[1]
    return picked_values.astype(jnp.int32)


def draw_kept_list_length(key, part):
    key = jax.random.fold_in(key, 12)
    first_key, second_key = jax.random.split(key)
    counts = jax.random.randint(first_key, (BOXES,), SK // 2, SK + 1)
    filled = jax.random.randint(second_key, (), 0, BOXES)
    return jnp.where(jnp.arange(BOXES) == filled, SK, counts).astype(jnp.int32)


def draw_ancestor_site_map(key, part):
    key = jax.random.fold_in(key, 13)
    column_keys = jax.random.split(key, COLUMNS)
    orders = jax.vmap(lambda single: jax.random.permutation(single, REGIONS * BOX_DEV))(column_keys)
    return orders.reshape(COLUMNS, REGIONS, BOX_DEV).transpose(1, 0, 2).reshape(BOXES).astype(jnp.int32)


def set_ends(values, key, low, largest):
    longest = values.shape.index(max(values.shape))
    spots = []
    for shift in (0, 1):
        where = [jax.random.randint(jax.random.fold_in(key, axis), (), 0, length) for axis, length in enumerate(values.shape)]
        where[longest] = (where[longest] + shift) % values.shape[longest]
        spots.append(tuple(where))
    return values.at[spots[0]].set(low).at[spots[1]].set(largest)


def levels(key, shape, cuts, smallest, largest):
    gain = 1.0
    for dim, blocks in cuts:
        heights = jax.random.uniform(jax.random.fold_in(jax.random.fold_in(key, 6), dim), (blocks,), jnp.float32, smallest / len(cuts), largest / len(cuts))
        gain = gain * jnp.repeat(jnp.exp(heights), shape[dim] // blocks).reshape((-1,) + (1,) * (len(shape) - 1 - dim))
    return gain


def gaussian(key, dims, width, bound, cuts=(), kind=jnp.bfloat16):
    values = width * jax.random.normal(key, dims, jnp.float32)
    if cuts:
        values = values * levels(key, dims, cuts, -0.22, 0.18)
    return jnp.clip(values, -bound, bound).astype(kind)


def setup_inputs(seed: int = 0) -> dict:
    arg_keys = jax.random.split(jax.random.key(seed), 11)
    kept_diagonal_tile = gaussian(arg_keys[0], (BOXES, S, S), 1.0, 6.0, ((0, 256),))
    discard_reciprocal = gaussian(arg_keys[1], (BOXES, R, R), R ** -0.5, 0.25, ((0, 256),))
    discard_by_kept = gaussian(arg_keys[2], (BOXES, R, S), 1.0, 6.0, ((0, 256),))
    kept_by_discard = gaussian(arg_keys[3], (BOXES, S, R), R ** -0.5, 0.25, ((0, 256),))
    adjacent_discard_to_kept = gaussian(arg_keys[4], (BOXES, NEAR, S, R), R ** -0.5, 0.25, ((0, 256),))
    adjacent_kept_to_discard = gaussian(arg_keys[5], (BOXES, NEAR, R, S), 1.0, 6.0, ((0, 256),))
    adjacent_site_table = set_ends(jax.random.randint(arg_keys[6], (BOXES, NEAR), 0, BOX_DEV + 1), jax.random.fold_in(arg_keys[6], 1), 0, BOX_DEV).astype(jnp.int32)
    retained_slots = draw_retained_slots(jax.random.fold_in(arg_keys[10], 71), 0)
    kept_list_length = draw_kept_list_length(jax.random.fold_in(arg_keys[10], 71), 0)
    ancestor_site_map = draw_ancestor_site_map(jax.random.fold_in(arg_keys[10], 71), 0)
    return {"kept_diagonal_tile": kept_diagonal_tile, "discard_reciprocal": discard_reciprocal, "discard_by_kept": discard_by_kept, "kept_by_discard": kept_by_discard, "adjacent_discard_to_kept": adjacent_discard_to_kept, "adjacent_kept_to_discard": adjacent_kept_to_discard, "adjacent_site_table": adjacent_site_table, "retained_slots": retained_slots, "kept_list_length": kept_list_length, "ancestor_site_map": ancestor_site_map}


offsets_list = (1, -1, 2, -2)


def device_side(pieces):
    skel, inverse_matrix, toward_skeleton, to_redund, left, right, slot = pieces
    places = skel.shape[0]
    solution_block = jnp.einsum("mjq,mqc->mjc", inverse_matrix.astype(jnp.float32), toward_skeleton.astype(jnp.float32)).astype(jnp.bfloat16)
    self_update = jnp.einsum("lsa,lat->lst", to_redund.astype(jnp.float32), solution_block.astype(jnp.float32))
    reduced = jnp.einsum("lab,lkbs->lkas", inverse_matrix.astype(jnp.float32), right.astype(jnp.float32)).astype(jnp.bfloat16)
    near_update = jnp.einsum("lksa,lkat->lkst", left.astype(jnp.float32), reduced.astype(jnp.float32))
    hits = slot[:, :, None] == jnp.arange(places, dtype=jnp.int32)[None, None, :]
    outgoing = jnp.sum(jnp.where(hits[:, :, :, None, None], near_update[:, :, None], jnp.float32(0.0)), axis=0)
    partial_block = skel.astype(jnp.float32) - self_update
    return partial_block, outgoing.astype(jnp.bfloat16)


def reference(kept_diagonal_tile, discard_reciprocal, discard_by_kept, kept_by_discard, adjacent_discard_to_kept, adjacent_kept_to_discard, adjacent_site_table, retained_slots, kept_list_length, ancestor_site_map):
    places = BOX_DEV
    devices = REGIONS * COLUMNS

    def split(array):
        return array.reshape((devices, places) + array.shape[1:])

    partial_block, outgoing = lax.map(device_side, (split(kept_diagonal_tile), split(discard_reciprocal), split(discard_by_kept), split(kept_by_discard), split(adjacent_discard_to_kept), split(adjacent_kept_to_discard), split(adjacent_site_table)))
    partial_block = partial_block.reshape(REGIONS, COLUMNS, places, S, S)
    outgoing = outgoing.reshape(REGIONS, COLUMNS, NEAR, places, S, S)
    refreshed_submatrix = partial_block
    for which, offset in enumerate(offsets_list):
        source = outgoing[:, :, which]
        blank = jnp.zeros((REGIONS, abs(offset), places, S, S), jnp.bfloat16)
        if offset > 0:
            moved = jnp.concatenate([blank, source[:, :COLUMNS - offset]], axis=1)
        else:
            moved = jnp.concatenate([source[:, -offset:], blank], axis=1)
        refreshed_submatrix = refreshed_submatrix - moved.astype(jnp.float32)
    refreshed_submatrix = refreshed_submatrix.reshape(BOXES, S, S)
    picked_values = jax.vmap(lambda dense_submatrix, element_slot: dense_submatrix[element_slot][:, element_slot])(refreshed_submatrix, retained_slots)
    valid = jnp.arange(SK, dtype=jnp.int32)[None, :] < kept_list_length[:, None]
    child = jnp.where(valid[:, :, None] & valid[:, None, :], picked_values, jnp.float32(0.0)).astype(jnp.bfloat16)
    child = child.reshape(REGIONS, COLUMNS, places, SK, SK).astype(jnp.float32)
    codes = ancestor_site_map.reshape(REGIONS, COLUMNS, places)
    hit = (codes[..., None] == jnp.arange(REGIONS * places, dtype=jnp.int32)).astype(jnp.float32)
    parent = jnp.einsum("rjlq,rjlxy->qjxy", hit, child, precision=lax.Precision.HIGHEST)
    parent = parent.reshape(REGIONS, places, COLUMNS, SK, SK).transpose(0, 2, 1, 3, 4)
    return parent.reshape(BOXES, SK, SK).astype(jnp.bfloat16)
```

```python
import functools

import jax
import jax.numpy as jnp
from jax import lax
from jax.experimental import pallas as pl
from jax.experimental.pallas import tpu as pltpu
from jax.sharding import PartitionSpec as P

offsets_list = (1, -1, 2, -2)
CODE_ROWS = 16
VMEM = pl.BlockSpec(memory_space=pltpu.VMEM)
HBM = pl.BlockSpec(memory_space=pltpu.HBM)
SMEM = pl.BlockSpec(memory_space=pltpu.SMEM)
LIMIT = 16 * 1024 * 1024
NEAR_LIMIT = 16 * 1024 * 1024


def shift(value, axis, by):
    length = lax.axis_size(axis)
    return lax.ppermute(value, axis, [(i, (i + by) % length) for i in range(length)])


def dot(a, b):
    return jnp.dot(a, b, preferred_element_type=jnp.float32)


def pickers(slots, span):
    count = slots.shape[1]
    column = lax.broadcasted_iota(jnp.int32, (span, count), 0) == slots
    tall = jnp.broadcast_to(slots, (128, count)).T
    lane = lax.broadcasted_iota(jnp.int32, (count, 128), 1)
    row = [tall == lane + at for at in range(0, span, 128)]
    one, zero = jnp.float32(1.0), jnp.float32(0.0)
    columns = jnp.where(column, one, zero).astype(jnp.bfloat16)
    rows = jnp.concatenate([jnp.where(r, one, zero).astype(jnp.bfloat16) for r in row], axis=1)
    return columns, rows


def self_kernel(slots_ref, tile_ref, inverse_ref, by_kept_ref, by_discard_ref, base_ref):
    place = pl.program_id(0)
    slots = jnp.where(place == 0, slots_ref[0:1, :], slots_ref[1:2, :])
    columns, rows = pickers(slots, tile_ref.shape[1])
    picked = dot(by_kept_ref[0], columns).astype(jnp.bfloat16)
    solved = dot(inverse_ref[0], picked).astype(jnp.bfloat16)
    left = dot(rows, by_discard_ref[0]).astype(jnp.bfloat16)
    tile = dot(rows, dot(tile_ref[0], columns).astype(jnp.bfloat16))
    base_ref[0] = tile - dot(left, solved)


def near_kernel(
    first,
    table_ref,
    one_ref,
    two_ref,
    inverse_ref,
    right_ref,
    left_ref,
    out_one,
    out_two,
    inverse,
    right,
    left,
    site_ref,
    sems,
):
    pairs = [(which, place) for which in range(2) for place in range(2)]
    copies = {}

    def copy(name, source, out):
        copies[name] = pltpu.make_async_copy(source, out, sems.at[len(copies)])
        copies[name].start()

    copy("site", table_ref, site_ref)
    for at, (which, place) in enumerate(pairs):
        copy(("right", at), right_ref.at[place, first + which], right.at[at])
    for place in range(2):
        copy(("inverse", place), inverse_ref.at[place], inverse.at[place])
    for at, (which, place) in enumerate(pairs):
        copy(("left", at), left_ref.at[place, first + which], left.at[at])

    copies["site"].wait()
    position = lax.axis_index("box")
    targets, columns, rows = [], [], []
    for which, place in pairs:
        there = position + offsets_list[first + which]
        inside = (there >= 0) & (there < lax.axis_size("box"))
        target = jnp.where(inside, site_ref[place, first + which], 2)
        slots_ref = (one_ref, two_ref)[which]
        column, row = pickers(
            jnp.where(target == 0, slots_ref[0:1], slots_ref[1:2]), left_ref.shape[2]
        )
        targets.append(target)
        columns.append(column)
        rows.append(row)

    for at in range(4):
        copies["right", at].wait()
    picked = [dot(right[at], columns[at]).astype(jnp.bfloat16) for at in range(4)]
    for place in range(2):
        copies["inverse", place].wait()
    reduced = [dot(inverse[place], picked[at]).astype(jnp.bfloat16) for at, (_, place) in enumerate(pairs)]
    for at in range(4):
        copies["left", at].wait()
    coupled = [dot(rows[at], left[at]).astype(jnp.bfloat16) for at in range(4)]
    near = [dot(coupled[at], reduced[at]) for at in range(4)]
    for which, out in enumerate((out_one, out_two)):
        for t in range(2):
            terms = [jnp.where(targets[2 * which + p] == t, near[2 * which + p], 0.0) for p in range(2)]
            out[t] = (terms[0] + terms[1]).astype(out.dtype)


def add_kernel(near_one, near_two, far_one, far_two, out_one, out_two):
    for near, far, out in ((near_one, far_one, out_one), (near_two, far_two, out_two)):
        out[...] = (near[...] + far[...].astype(jnp.float32)).astype(jnp.bfloat16)


def child_kernel(length_ref, code_ref, base_ref, a_ref, b_ref, out_ref):
    span = base_ref.shape[1]
    for place in range(base_ref.shape[0]):
        value = base_ref[place]
        for ref in (a_ref, b_ref):
            value = value - ref[place].astype(jnp.float32)
        length = length_ref[place]
        row = lax.broadcasted_iota(jnp.int32, (span, span), 0)
        column = lax.broadcasted_iota(jnp.int32, (span, span), 1)
        valid = (row < length) & (column < length)
        out_ref[place, 0:span] = jnp.where(valid, value, 0.0).astype(jnp.bfloat16)
        code = code_ref[place].astype(jnp.float32)
        out_ref[place, span:] = jnp.full((CODE_ROWS, span), code, jnp.float32).astype(jnp.bfloat16)


def choose_kernel(a_ref, b_ref, c_ref, d_ref, mine_ref, other_ref):
    span = mine_ref.shape[1]
    region = lax.axis_index("region")
    partner = region + 1 - 2 * lax.rem(region, 2)
    for out_ref, owner in ((mine_ref, region), (other_ref, partner)):
        for slot in range(2):
            wanted = (owner * 2 + slot).astype(jnp.float32)
            value = None
            for ref in (a_ref, b_ref, c_ref, d_ref):
                for place in range(2):
                    code = ref[place, span : span + 1, :].astype(jnp.float32)
                    hit = jnp.where(code == wanted, 1.0, 0.0).astype(jnp.bfloat16)
                    term = ref[place, 0:span] * hit
                    value = term if value is None else value + term
            out_ref[slot] = value


def join_kernel(a_ref, b_ref, out_ref):
    out_ref[...] = a_ref[...] + b_ref[...]


def local(
    kept_diagonal_tile,
    discard_reciprocal,
    discard_by_kept,
    kept_by_discard,
    adjacent_discard_to_kept,
    adjacent_kept_to_discard,
    adjacent_site_table,
    retained_slots,
    kept_list_length,
    ancestor_site_map,
):
    places, tile_span = retained_slots.shape
    wide, tall = kept_diagonal_tile.shape[1], discard_reciprocal.shape[1]
    params = pltpu.CompilerParams(vmem_limit_bytes=LIMIT)
    small = jax.ShapeDtypeStruct((places, tile_span, tile_span), jnp.bfloat16)

    def block(rows, columns):
        return pl.BlockSpec((1, rows, columns), lambda l: (l, 0, 0))

    def self_update():
        return pl.pallas_call(
            self_kernel,
            grid=(places,),
            in_specs=[VMEM, block(wide, wide), block(tall, tall), block(tall, wide), block(wide, tall)],
            out_specs=block(tile_span, tile_span),
            out_shape=jax.ShapeDtypeStruct((places, tile_span, tile_span), jnp.float32),
            compiler_params=params,
            name="self_update",
        )(retained_slots, kept_diagonal_tile, discard_reciprocal, discard_by_kept, kept_by_discard)

    def slots_of(first):
        return [shift(retained_slots, "box", -offsets_list[first + i]) for i in range(2)]

    def near(first, slots, dtype):
        shape = jax.ShapeDtypeStruct((places, tile_span, tile_span), dtype)
        return pl.pallas_call(
            functools.partial(near_kernel, first),
            in_specs=[HBM, VMEM, VMEM, HBM, HBM, HBM],
            out_specs=[VMEM, VMEM],
            out_shape=[shape, shape],
            scratch_shapes=[
                pltpu.VMEM((2, tall, tall), jnp.bfloat16),
                pltpu.VMEM((4, tall, wide), jnp.bfloat16),
                pltpu.VMEM((4, wide, tall), jnp.bfloat16),
                pltpu.SMEM(adjacent_site_table.shape, jnp.int32),
                pltpu.SemaphoreType.DMA((11,)),
            ],
            compiler_params=pltpu.CompilerParams(vmem_limit_bytes=NEAR_LIMIT),
            name="near_update",
        )(
            pltpu.with_memory_space_constraint(adjacent_site_table, pltpu.HBM),
            *slots,
            *[pltpu.with_memory_space_constraint(v, pltpu.HBM) for v in (discard_reciprocal, adjacent_kept_to_discard, adjacent_discard_to_kept)],
        )

    far_slots, near_slots = lax.optimization_barrier((slots_of(2), slots_of(0)))
    far_one, far_two = near(2, far_slots, jnp.bfloat16)
    passed = [shift(far_one, "box", 1), shift(far_two, "box", -1)]
    near_one, near_two = near(0, near_slots, jnp.float32)
    sent = pl.pallas_call(
        add_kernel,
        in_specs=[VMEM] * 4,
        out_specs=[VMEM] * 2,
        out_shape=[small, small],
        compiler_params=params,
        name="add",
    )(near_one, near_two, *passed)
    arrived = [shift(sent[0], "box", 1), shift(sent[1], "box", -1)]
    base = self_update()

    child = pl.pallas_call(
        child_kernel,
        in_specs=[SMEM, SMEM] + [VMEM] * 3,
        out_specs=VMEM,
        out_shape=jax.ShapeDtypeStruct((places, tile_span + CODE_ROWS, tile_span), jnp.bfloat16),
        compiler_params=params,
        name="child",
    )(kept_list_length, ancestor_site_map, base, *arrived)

    gathered = [child] + [shift(child, "region", by) for by in (2, -2, 4)]
    mine, other = pl.pallas_call(
        choose_kernel,
        in_specs=[VMEM] * 4,
        out_specs=[VMEM, VMEM],
        out_shape=[small, small],
        compiler_params=params,
        name="choose",
    )(*gathered)
    partners = [(i, i ^ 1) for i in range(lax.axis_size("region"))]
    received = lax.ppermute(other, "region", partners)
    return pl.pallas_call(
        join_kernel,
        in_specs=[VMEM] * 2,
        out_specs=VMEM,
        out_shape=small,
        compiler_params=params,
        name="join",
    )(mine, received)


def solution(mesh):
    in_specs = (
        P(("region", "box"), None, None),
        P(("region", "box"), None, None),
        P(("region", "box"), None, None),
        P(("region", "box"), None, None),
        P(("region", "box"), None, None, None),
        P(("region", "box"), None, None, None),
        P(("region", "box"), None),
        P(("region", "box"), None),
        P(("region", "box")),
        P(("region", "box")),
    )
    out_specs = P(("region", "box"), None, None)
    return jax.shard_map(local, mesh=mesh, in_specs=in_specs, out_specs=out_specs, check_vma=False)
```

```python
import functools

import jax
import jax.numpy as jnp
from jax import lax
from jax.experimental import pallas as pl
from jax.experimental.pallas import tpu as pltpu
from jax.sharding import PartitionSpec as P

offsets_list = (1, -1, 2, -2)
CODE_ROWS = 16
VMEM = pl.BlockSpec(memory_space=pltpu.VMEM)
HBM = pl.BlockSpec(memory_space=pltpu.HBM)
SMEM = pl.BlockSpec(memory_space=pltpu.SMEM)
LIMIT = 16 * 1024 * 1024
NEAR_LIMIT = 16 * 1024 * 1024


def shift(value, axis, by):
    length = lax.axis_size(axis)
    return lax.ppermute(value, axis, [(i, (i + by) % length) for i in range(length)])


def turn(value, by):
    regions, length = lax.axis_size("region"), lax.axis_size("box")
    pairs = []
    for r in range(regions):
        for j in range(length):
            there = j + (by if r % 2 == 0 else -by)
            goal = (r, there) if 0 <= there < length else (r + 1 - 2 * (r % 2), j)
            pairs.append((r * length + j, goal[0] * length + goal[1]))
    return lax.ppermute(value, ("region", "box"), pairs)


def dot(a, b):
    return jnp.dot(a, b, preferred_element_type=jnp.float32)


def pickers(slots, span):
    count = slots.shape[1]
    column = lax.broadcasted_iota(jnp.int32, (span, count), 0) == slots
    tall = jnp.broadcast_to(slots, (128, count)).T
    lane = lax.broadcasted_iota(jnp.int32, (count, 128), 1)
    row = [tall == lane + at for at in range(0, span, 128)]
    one, zero = jnp.float32(1.0), jnp.float32(0.0)
    columns = jnp.where(column, one, zero).astype(jnp.bfloat16)
    rows = jnp.concatenate([jnp.where(r, one, zero).astype(jnp.bfloat16) for r in row], axis=1)
    return columns, rows


def self_kernel(slots_ref, tile_ref, inverse_ref, by_kept_ref, by_discard_ref, base_ref):
    place = pl.program_id(0)
    slots = jnp.where(place == 0, slots_ref[0:1, :], slots_ref[1:2, :])
    columns, rows = pickers(slots, tile_ref.shape[1])
    picked = dot(by_kept_ref[0], columns).astype(jnp.bfloat16)
    solved = dot(inverse_ref[0], picked).astype(jnp.bfloat16)
    left = dot(rows, by_discard_ref[0]).astype(jnp.bfloat16)
    tile = dot(rows, dot(tile_ref[0], columns).astype(jnp.bfloat16))
    base_ref[0] = tile - dot(left, solved)


def directions():
    core = lax.rem(lax.axis_index("region"), 2)
    return core, 1 - core


def load_kernel(first, *refs):
    count = (len(refs) - 1) // 2
    sources, outs, sems = refs[:count], refs[count : 2 * count], refs[2 * count]
    copies = []

    def copy(source, out):
        copies.append(pltpu.make_async_copy(source, out, sems.at[len(copies)]))

    along = directions()
    for source, out in zip(sources, outs):
        if len(source.shape) == 4:
            for which in range(2):
                for place in range(2):
                    copy(source.at[place, first + along[which]], out.at[2 * which + place])
        else:
            copy(source, out)
    for each in copies:
        each.start()
    for each in copies:
        each.wait()


def near_kernel(first, span, slots_of, site_ref, inverse, right, left):
    along = directions()
    core = along[0]
    position = lax.axis_index("box")
    pairs = [(which, place) for which in range(2) for place in range(2)]
    targets, columns, rows = [], [], []
    for which, place in pairs:
        there = position + offsets_list[first] * (1 - 2 * along[which])
        inside = (there >= 0) & (there < lax.axis_size("box"))
        one, two = (site_ref[place : place + 1, first + i : first + i + 1] for i in (which, 1 - which))
        target = jnp.where(inside, jnp.where(core == 0, one, two), 2)
        slots = slots_of(which)
        column, row = pickers(jnp.where(target == 0, slots[0:1], slots[1:2]), span)
        targets.append(target)
        columns.append(column)
        rows.append(row)
    picked = [dot(right[at], columns[at]).astype(jnp.bfloat16) for at in range(4)]
    reduced = [dot(inverse[place], picked[at]).astype(jnp.bfloat16) for at, (_, place) in enumerate(pairs)]
    coupled = [dot(rows[at], left[at]).astype(jnp.bfloat16) for at in range(4)]
    near = [dot(coupled[at], reduced[at]) for at in range(4)]
    return [
        [sum(jnp.where(targets[2 * which + p] == t, near[2 * which + p], 0.0) for p in range(2)) for t in range(2)]
        for which in range(2)
    ]


def far_kernel(one_ref, two_ref, own_ref, site_ref, inverse, right, left, out_one, out_two):
    span = own_ref.shape[1]
    from_there = (two_ref, one_ref)
    updates = near_kernel(2, left.shape[1], lambda w: from_there[w][...], site_ref, inverse, right, left)
    own = own_ref[...]
    row = lax.broadcasted_iota(jnp.int32, (CODE_ROWS, span), 0)
    halves = (own >> 1, own & 1)
    code = jnp.zeros((CODE_ROWS, span), jnp.int32)
    for at in range(4):
        code = jnp.where(row == at, halves[at // 2][at % 2 : at % 2 + 1], code)
    code = code.astype(jnp.float32).astype(jnp.bfloat16)
    for out, update in zip((out_one, out_two), updates):
        for t in range(2):
            out[t * span : (t + 1) * span] = update[t].astype(jnp.bfloat16)
        out[2 * span :] = code


def step_kernel(one_ref, two_ref, site_ref, inverse, right, left, out_one, out_two):
    span = out_one.shape[1]
    passed = (one_ref, two_ref)

    def slots_of(which):
        code = passed[1 - which][2 * span :].astype(jnp.float32).astype(jnp.int32)
        return code[0:2] * 2 + code[2:4]

    updates = near_kernel(0, left.shape[1], slots_of, site_ref, inverse, right, left)
    for which, out in enumerate((out_one, out_two)):
        for t in range(2):
            far = passed[which][t * span : (t + 1) * span].astype(jnp.float32)
            out[t] = (updates[which][t] + far).astype(jnp.bfloat16)


def child_kernel(length_ref, code_ref, base_ref, a_ref, b_ref, out_ref):
    span = base_ref.shape[1]
    for place in range(base_ref.shape[0]):
        value = base_ref[place]
        for ref in (a_ref, b_ref):
            value = value - ref[place].astype(jnp.float32)
        length = length_ref[place]
        row = lax.broadcasted_iota(jnp.int32, (span, span), 0)
        column = lax.broadcasted_iota(jnp.int32, (span, span), 1)
        valid = (row < length) & (column < length)
        out_ref[place * span : (place + 1) * span] = jnp.where(valid, value, 0.0).astype(jnp.bfloat16)
    row = lax.broadcasted_iota(jnp.int32, (CODE_ROWS, span), 0)
    code = jnp.where(row == 0, code_ref[0], code_ref[1])
    out_ref[2 * span :] = code.astype(jnp.float32).astype(jnp.bfloat16)


def choose_kernel(a_ref, b_ref, c_ref, d_ref, mine_ref, other_ref):
    span = mine_ref.shape[1]
    region = lax.axis_index("region")
    partner = region + 1 - 2 * lax.rem(region, 2)
    for out_ref, owner in ((mine_ref, region), (other_ref, partner)):
        for slot in range(2):
            wanted = (owner * 2 + slot).astype(jnp.float32)
            value = None
            for ref in (a_ref, b_ref, c_ref, d_ref):
                for place in range(2):
                    code = ref[2 * span :].astype(jnp.float32)[place : place + 1]
                    hit = jnp.where(code == wanted, 1.0, 0.0).astype(jnp.bfloat16)
                    term = ref[place * span : (place + 1) * span] * hit
                    value = term if value is None else value + term
            out_ref[slot] = value


def join_kernel(a_ref, b_ref, out_ref):
    out_ref[...] = a_ref[...] + b_ref[...]


def local(
    kept_diagonal_tile,
    discard_reciprocal,
    discard_by_kept,
    kept_by_discard,
    adjacent_discard_to_kept,
    adjacent_kept_to_discard,
    adjacent_site_table,
    retained_slots,
    kept_list_length,
    ancestor_site_map,
):
    places, tile_span = retained_slots.shape
    wide, tall = kept_diagonal_tile.shape[1], discard_reciprocal.shape[1]
    params = pltpu.CompilerParams(vmem_limit_bytes=LIMIT)
    small = jax.ShapeDtypeStruct((places, tile_span, tile_span), jnp.bfloat16)

    def block(rows, columns):
        return pl.BlockSpec((1, rows, columns), lambda l: (l, 0, 0))

    own = (retained_slots, kept_diagonal_tile, discard_reciprocal, discard_by_kept, kept_by_discard)

    def self_update(*own):
        return pl.pallas_call(
            self_kernel,
            grid=(places,),
            in_specs=[VMEM, block(wide, wide), block(tall, tall), block(tall, wide), block(wide, tall)],
            out_specs=block(tile_span, tile_span),
            out_shape=jax.ShapeDtypeStruct((places, tile_span, tile_span), jnp.float32),
            compiler_params=params,
            name="self_update",
        )(*own)

    def load(first, sources):
        shapes = [(4,) + v.shape[2:] if v.ndim == 4 else v.shape for v in sources]
        return pl.pallas_call(
            functools.partial(load_kernel, first),
            in_specs=[HBM] * len(sources),
            out_specs=[VMEM] * len(sources),
            out_shape=[pltpu.VMEM(shape, v.dtype) for shape, v in zip(shapes, sources)],
            scratch_shapes=[pltpu.SemaphoreType.DMA((12,))],
            compiler_params=params,
            name="load",
        )(*[pltpu.with_memory_space_constraint(v, pltpu.HBM) for v in sources])

    coupled = (adjacent_kept_to_discard, adjacent_discard_to_kept)
    far_slots = [turn(retained_slots, by) for by in (2, -2)]
    site, inverse, *far_pair = load(2, (adjacent_site_table, discard_reciprocal) + coupled)
    message = jax.ShapeDtypeStruct((places * tile_span + CODE_ROWS, tile_span), jnp.bfloat16)
    far = pl.pallas_call(
        far_kernel,
        in_specs=[VMEM] * 7,
        out_specs=[VMEM] * 2,
        out_shape=[message] * 2,
        compiler_params=params,
        name="far_update",
    )(*far_slots, retained_slots, site, inverse, *far_pair)
    passed = [turn(value, by) for value, by in zip(far, (1, -1))]
    coupled, own, far = lax.optimization_barrier((coupled, own, far))
    near_pair = load(0, coupled)
    sent = pl.pallas_call(
        step_kernel,
        in_specs=[VMEM] * 6,
        out_specs=[VMEM] * 2,
        out_shape=[small, small],
        compiler_params=params,
        name="near_update",
    )(*passed, site, inverse, *near_pair)
    arrived = [turn(sent[0], 1), turn(sent[1], -1)]
    base = self_update(*own)

    child = pl.pallas_call(
        child_kernel,
        in_specs=[SMEM, SMEM] + [VMEM] * 3,
        out_specs=VMEM,
        out_shape=message,
        compiler_params=params,
        name="child",
    )(kept_list_length, ancestor_site_map, base, *arrived)

    gathered = [child] + [shift(child, "region", by) for by in (4, 2, -2)]
    mine, other = pl.pallas_call(
        choose_kernel,
        in_specs=[VMEM] * 4,
        out_specs=[VMEM, VMEM],
        out_shape=[small, small],
        compiler_params=params,
        name="choose",
    )(*gathered)
    partners = [(i, i ^ 1) for i in range(lax.axis_size("region"))]
    received = lax.ppermute(other, "region", partners)
    return pl.pallas_call(
        join_kernel,
        in_specs=[VMEM] * 2,
        out_specs=VMEM,
        out_shape=small,
        compiler_params=params,
        name="join",
    )(mine, received)


def solution(mesh):
    in_specs = (
        P(("region", "box"), None, None),
        P(("region", "box"), None, None),
        P(("region", "box"), None, None),
        P(("region", "box"), None, None),
        P(("region", "box"), None, None, None),
        P(("region", "box"), None, None, None),
        P(("region", "box"), None),
        P(("region", "box"), None),
        P(("region", "box")),
        P(("region", "box")),
    )
    out_specs = P(("region", "box"), None, None)
    return jax.shard_map(local, mesh=mesh, in_specs=in_specs, out_specs=out_specs, check_vma=False)
```

```python
import functools

import jax
import jax.numpy as jnp
from jax import lax
from jax.experimental import pallas as pl
from jax.experimental.pallas import tpu as pltpu
from jax.sharding import PartitionSpec as P

offsets_list = (1, -1, 2, -2)
CODE_ROWS = 16
VMEM = pl.BlockSpec(memory_space=pltpu.VMEM)
HBM = pl.BlockSpec(memory_space=pltpu.HBM)
SMEM = pl.BlockSpec(memory_space=pltpu.SMEM)
LIMIT = 16 * 1024 * 1024
NEAR_LIMIT = 16 * 1024 * 1024


def shift(value, axis, by):
    length = lax.axis_size(axis)
    return lax.ppermute(value, axis, [(i, (i + by) % length) for i in range(length)])


def turn(value, by):
    regions, length = lax.axis_size("region"), lax.axis_size("box")
    pairs = []
    for r in range(regions):
        for j in range(length):
            there = j + (by if r % 2 == 0 else -by)
            goal = (r, there) if 0 <= there < length else (r + 1 - 2 * (r % 2), j)
            pairs.append((r * length + j, goal[0] * length + goal[1]))
    return lax.ppermute(value, ("region", "box"), pairs)


def dot(a, b):
    return jnp.dot(a, b, preferred_element_type=jnp.float32)


def pickers(slots, span):
    count = slots.shape[1]
    column = lax.broadcasted_iota(jnp.int32, (span, count), 0) == slots
    tall = jnp.broadcast_to(slots, (128, count)).T
    lane = lax.broadcasted_iota(jnp.int32, (count, 128), 1)
    row = [tall == lane + at for at in range(0, span, 128)]
    one, zero = jnp.float32(1.0), jnp.float32(0.0)
    columns = jnp.where(column, one, zero).astype(jnp.bfloat16)
    rows = jnp.concatenate([jnp.where(r, one, zero).astype(jnp.bfloat16) for r in row], axis=1)
    return columns, rows


def self_kernel(slots_ref, tile_ref, inverse_ref, by_kept_ref, by_discard_ref, base_ref):
    place = pl.program_id(0)
    slots = jnp.where(place == 0, slots_ref[0:1, :], slots_ref[1:2, :])
    columns, rows = pickers(slots, tile_ref.shape[1])
    picked = dot(by_kept_ref[0], columns).astype(jnp.bfloat16)
    solved = dot(inverse_ref[0], picked).astype(jnp.bfloat16)
    left = dot(rows, by_discard_ref[0]).astype(jnp.bfloat16)
    tile = dot(rows, dot(tile_ref[0], columns).astype(jnp.bfloat16))
    base_ref[0] = tile - dot(left, solved)


def directions():
    core = lax.rem(lax.axis_index("region"), 2)
    return core, 1 - core


def load_kernel(first, *refs):
    count = (len(refs) - 1) // 2
    sources, outs, sems = refs[:count], refs[count : 2 * count], refs[2 * count]
    copies = []
    for source, out in zip(sources, outs):
        for piece, target in pieces(first, source, out):
            copies.append(pltpu.make_async_copy(piece, target, sems.at[len(copies)]))
    for each in copies:
        each.start()
    for each in copies:
        each.wait()


def pieces(first, source, out):
    if len(source.shape) != 4:
        return [(source, out)]
    along = directions()
    return [
        (source.at[place, first + along[which]], out.at[2 * which + place])
        for which in range(2)
        for place in range(2)
    ]


def reduce_kernel(
    first, table_ref, inverse_ref, right_ref, left_ref, site, inverse, reduced, left, right, sems
):
    early, late = [], []
    for group, source, out in (
        (early, right_ref, right),
        (early, inverse_ref, inverse),
        (late, left_ref, left),
        (late, table_ref, site),
    ):
        for piece, target in pieces(first, source, out):
            group.append(pltpu.make_async_copy(piece, target, sems.at[len(early) + len(late)]))
    for each in early + late:
        each.start()
    for each in early:
        each.wait()
    for at in range(4):
        reduced[at] = dot(inverse[at % 2], right[at]).astype(jnp.bfloat16)
    for each in late:
        each.wait()


def targets_of(first, site_ref):
    along = directions()
    position = lax.axis_index("box")
    targets = []
    for which in range(2):
        there = position + offsets_list[first] * (1 - 2 * along[which])
        inside = (there >= 0) & (there < lax.axis_size("box"))
        row = []
        for place in range(2):
            one, two = (site_ref[place : place + 1, first + i : first + i + 1] for i in (which, 1 - which))
            row.append(jnp.where(inside, jnp.where(along[0] == 0, one, two), 2))
        targets.append(row)
    return targets


def join_places(targets, near):
    return [
        [sum(jnp.where(targets[w][p] == t, near[2 * w + p], 0.0) for p in range(2)) for t in range(2)]
        for w in range(2)
    ]


def whole_kernel(site_ref, inverse, right, left, out):
    reduced = [dot(inverse[at % 2], right[at]).astype(jnp.bfloat16) for at in range(4)]
    near = [dot(left[at], reduced[at]) for at in range(4)]
    sums = join_places(targets_of(0, site_ref), near)
    for which in range(2):
        for t in range(2):
            out[2 * which + t] = sums[which][t].astype(jnp.bfloat16)


def far_kernel(one_ref, two_ref, own_ref, site_ref, reduced, left, out_one, out_two):
    span = own_ref.shape[1]
    from_there = (two_ref[...], one_ref[...])
    targets = targets_of(2, site_ref)
    picks = []
    for which in range(2):
        slots = from_there[which]
        for place in range(2):
            own_slots = jnp.where(targets[which][place] == 0, slots[0:1], slots[1:2])
            picks.append(pickers(own_slots, left.shape[1]))
    picked = [dot(reduced[at], picks[at][0]).astype(jnp.bfloat16) for at in range(4)]
    coupled = [dot(picks[at][1], left[at]).astype(jnp.bfloat16) for at in range(4)]
    near = [dot(coupled[at], picked[at]) for at in range(4)]
    updates = join_places(targets, near)
    own = own_ref[...]
    row = lax.broadcasted_iota(jnp.int32, (CODE_ROWS, span), 0)
    halves = (own >> 1, own & 1)
    code = jnp.zeros((CODE_ROWS, span), jnp.int32)
    for at in range(4):
        code = jnp.where(row == at, halves[at // 2][at % 2 : at % 2 + 1], code)
    code = code.astype(jnp.float32).astype(jnp.bfloat16)
    for out, update in zip((out_one, out_two), updates):
        for t in range(2):
            out[t * span : (t + 1) * span] = update[t].astype(jnp.bfloat16)
        out[2 * span :] = code


def step_kernel(one_ref, two_ref, near_ref, out_one, out_two):
    span = out_one.shape[1]
    passed = (one_ref, two_ref)
    picks = []
    for which in range(2):
        code = passed[1 - which][2 * span :].astype(jnp.float32).astype(jnp.int32)
        slots = code[0:2] * 2 + code[2:4]
        picks += [pickers(slots[t : t + 1], near_ref.shape[1]) for t in range(2)]
    half = [dot(near_ref[at], picks[at][0]).astype(jnp.bfloat16) for at in range(4)]
    near = [dot(picks[at][1], half[at]) for at in range(4)]
    for which, out in enumerate((out_one, out_two)):
        for t in range(2):
            far = passed[which][t * span : (t + 1) * span].astype(jnp.float32)
            out[t] = (near[2 * which + t] + far).astype(jnp.bfloat16)


def child_kernel(length_ref, code_ref, base_ref, one_ref, two_ref, *outs):
    places, span = base_ref.shape[:2]
    row = lax.broadcasted_iota(jnp.int32, (span, span), 0)
    column = lax.broadcasted_iota(jnp.int32, (span, span), 1)
    for place in range(places):
        value = base_ref[place] - one_ref[place].astype(jnp.float32) - two_ref[place].astype(jnp.float32)
        length = length_ref[place]
        valid = (row < length) & (column < length)
        outs[place][0:span] = jnp.where(valid, value, 0.0).astype(jnp.bfloat16)
    row = lax.broadcasted_iota(jnp.int32, (CODE_ROWS, span), 0)
    code = jnp.where(row == 0, code_ref[0], code_ref[1])
    outs[0][span:] = code.astype(jnp.float32).astype(jnp.bfloat16)


def choose_kernel(*refs):
    sources, (mine_ref, other_ref) = refs[:-2], refs[-2:]
    children = (sources[: len(sources) // 2], sources[len(sources) // 2 :])
    span = mine_ref.shape[1]
    region = lax.axis_index("region")
    partner = region + 1 - 2 * lax.rem(region, 2)
    codes = [ref[span:].astype(jnp.float32) for ref in children[0]]
    for out_ref, owner in ((mine_ref, region), (other_ref, partner)):
        for slot in range(2):
            wanted = (owner * 2 + slot).astype(jnp.float32)
            value = None
            for place in range(2):
                for ref, code in zip(children[place], codes):
                    hit = jnp.where(code[place : place + 1] == wanted, 1.0, 0.0).astype(jnp.bfloat16)
                    term = ref[0:span] * hit
                    value = term if value is None else value + term
            out_ref[slot] = value


def join_kernel(a_ref, b_ref, out_ref):
    out_ref[...] = a_ref[...] + b_ref[...]


def local(
    kept_diagonal_tile,
    discard_reciprocal,
    discard_by_kept,
    kept_by_discard,
    adjacent_discard_to_kept,
    adjacent_kept_to_discard,
    adjacent_site_table,
    retained_slots,
    kept_list_length,
    ancestor_site_map,
):
    places, tile_span = retained_slots.shape
    wide, tall = kept_diagonal_tile.shape[1], discard_reciprocal.shape[1]
    params = pltpu.CompilerParams(vmem_limit_bytes=LIMIT)
    small = jax.ShapeDtypeStruct((places, tile_span, tile_span), jnp.bfloat16)

    def block(rows, columns):
        return pl.BlockSpec((1, rows, columns), lambda l: (l, 0, 0))

    own = (retained_slots, kept_diagonal_tile, discard_reciprocal, discard_by_kept, kept_by_discard)

    def self_update(*own):
        return pl.pallas_call(
            self_kernel,
            grid=(places,),
            in_specs=[VMEM, block(wide, wide), block(tall, tall), block(tall, wide), block(wide, tall)],
            out_specs=block(tile_span, tile_span),
            out_shape=jax.ShapeDtypeStruct((places, tile_span, tile_span), jnp.float32),
            compiler_params=params,
            name="self_update",
        )(*own)

    def load(first, sources):
        shapes = [(4,) + v.shape[2:] if v.ndim == 4 else v.shape for v in sources]
        return pl.pallas_call(
            functools.partial(load_kernel, first),
            in_specs=[HBM] * len(sources),
            out_specs=[VMEM] * len(sources),
            out_shape=[pltpu.VMEM(shape, v.dtype) for shape, v in zip(shapes, sources)],
            scratch_shapes=[pltpu.SemaphoreType.DMA((8,))],
            compiler_params=params,
            name="load",
        )(*[pltpu.with_memory_space_constraint(v, pltpu.HBM) for v in sources])

    coupled = (adjacent_kept_to_discard, adjacent_discard_to_kept)
    far_slots = [turn(retained_slots, by) for by in (2, -2)]
    far_sources = (adjacent_site_table, discard_reciprocal) + coupled
    rights, lefts = (4, tall, wide), (4, wide, tall)
    site, inverse, reduced, far_left = pl.pallas_call(
        functools.partial(reduce_kernel, 2),
        in_specs=[HBM] * 4,
        out_specs=[VMEM] * 4,
        out_shape=[
            pltpu.VMEM(adjacent_site_table.shape, jnp.int32),
            pltpu.VMEM(discard_reciprocal.shape, jnp.bfloat16),
            pltpu.VMEM(rights, jnp.bfloat16),
            pltpu.VMEM(lefts, jnp.bfloat16),
        ],
        scratch_shapes=[pltpu.VMEM(rights, jnp.bfloat16), pltpu.SemaphoreType.DMA((10,))],
        compiler_params=params,
        name="load_reduce",
    )(*[pltpu.with_memory_space_constraint(v, pltpu.HBM) for v in far_sources])
    message = jax.ShapeDtypeStruct((places * tile_span + CODE_ROWS, tile_span), jnp.bfloat16)
    far = pl.pallas_call(
        far_kernel,
        in_specs=[VMEM] * 6,
        out_specs=[VMEM] * 2,
        out_shape=[message] * 2,
        compiler_params=params,
        name="far_update",
    )(*far_slots, retained_slots, site, reduced, far_left)
    passed = [turn(value, by) for value, by in zip(far, (1, -1))]
    coupled, own, far = lax.optimization_barrier((coupled, own, far))
    near_pair = load(0, coupled)
    whole = pl.pallas_call(
        whole_kernel,
        in_specs=[VMEM] * 4,
        out_specs=VMEM,
        out_shape=jax.ShapeDtypeStruct((4, wide, wide), jnp.bfloat16),
        compiler_params=params,
        name="whole_update",
    )(site, inverse, *near_pair)
    sent = pl.pallas_call(
        step_kernel,
        in_specs=[VMEM] * 3,
        out_specs=[VMEM] * 2,
        out_shape=[small, small],
        compiler_params=params,
        name="near_update",
    )(*passed, whole)
    arrived = [turn(sent[0], 1), turn(sent[1], -1)]
    base = self_update(*own)

    half = jax.ShapeDtypeStruct((tile_span, tile_span), jnp.bfloat16)
    coded = jax.ShapeDtypeStruct((tile_span + CODE_ROWS, tile_span), jnp.bfloat16)
    one, two = pl.pallas_call(
        child_kernel,
        in_specs=[SMEM, SMEM] + [VMEM] * 3,
        out_specs=[VMEM] * 2,
        out_shape=[coded, half],
        compiler_params=params,
        name="child",
    )(kept_list_length, ancestor_site_map, base, *arrived)

    one_back, two_ahead = shift(one, "region", 2), shift(two, "region", -2)
    two_back, one_ahead = shift(two, "region", 2), shift(one, "region", -2)
    one_far, two_far = shift(one_back, "region", 2), shift(two_ahead, "region", -2)
    gathered = [one, one_back, one_ahead, one_far, two, two_back, two_ahead, two_far]
    mine, other = pl.pallas_call(
        choose_kernel,
        in_specs=[VMEM] * 8,
        out_specs=[VMEM, VMEM],
        out_shape=[small, small],
        compiler_params=params,
        name="choose",
    )(*gathered)
    partners = [(i, i ^ 1) for i in range(lax.axis_size("region"))]
    received = lax.ppermute(other, "region", partners)
    return pl.pallas_call(
        join_kernel,
        in_specs=[VMEM] * 2,
        out_specs=VMEM,
        out_shape=small,
        compiler_params=params,
        name="join",
    )(mine, received)


def solution(mesh):
    in_specs = (
        P(("region", "box"), None, None),
        P(("region", "box"), None, None),
        P(("region", "box"), None, None),
        P(("region", "box"), None, None),
        P(("region", "box"), None, None, None),
        P(("region", "box"), None, None, None),
        P(("region", "box"), None),
        P(("region", "box"), None),
        P(("region", "box")),
        P(("region", "box")),
    )
    out_specs = P(("region", "box"), None, None)
    return jax.shard_map(local, mesh=mesh, in_specs=in_specs, out_specs=out_specs, check_vma=False)
```

```python
import functools

import jax
import jax.numpy as jnp
from jax import lax
from jax.experimental import pallas as pl
from jax.experimental.pallas import tpu as pltpu
from jax.sharding import PartitionSpec as P

offsets_list = (1, -1, 2, -2)
CODE_ROWS = 16
VMEM = pl.BlockSpec(memory_space=pltpu.VMEM)
HBM = pl.BlockSpec(memory_space=pltpu.HBM)
SMEM = pl.BlockSpec(memory_space=pltpu.SMEM)
LIMIT = 16 * 1024 * 1024
NEAR_LIMIT = 16 * 1024 * 1024


def shift(value, axis, by):
    length = lax.axis_size(axis)
    return lax.ppermute(value, axis, [(i, (i + by) % length) for i in range(length)])


def swap(value, by, parity):
    regions, length = lax.axis_size("region"), lax.axis_size("box")
    pairs = []
    for r in range(regions):
        for j in range(length):
            there = j + by if j // by % 2 == parity else j - by
            goal = (r, there) if 0 <= there < length else (r + 1 - 2 * (r % 2), j)
            pairs.append((r * length + j, goal[0] * length + goal[1]))
    return lax.ppermute(value, ("region", "box"), pairs)


def dot(a, b):
    return jnp.dot(a, b, preferred_element_type=jnp.float32)


def pickers(slots, span):
    count = slots.shape[1]
    column = lax.broadcasted_iota(jnp.int32, (span, count), 0) == slots
    tall = jnp.broadcast_to(slots, (128, count)).T
    lane = lax.broadcasted_iota(jnp.int32, (count, 128), 1)
    row = [tall == lane + at for at in range(0, span, 128)]
    one, zero = jnp.float32(1.0), jnp.float32(0.0)
    columns = jnp.where(column, one, zero).astype(jnp.bfloat16)
    rows = jnp.concatenate([jnp.where(r, one, zero).astype(jnp.bfloat16) for r in row], axis=1)
    return columns, rows


def self_kernel(
    length_ref, code_ref, slots_ref, tile_ref, inverse_ref, by_kept_ref, by_discard_ref, base_ref, keep_ref, codes_ref
):
    place = pl.program_id(0)
    slots = jnp.where(place == 0, slots_ref[0:1, :], slots_ref[1:2, :])
    columns, rows = pickers(slots, tile_ref.shape[1])
    picked = dot(by_kept_ref[0], columns).astype(jnp.bfloat16)
    solved = dot(inverse_ref[0], picked).astype(jnp.bfloat16)
    left = dot(rows, by_discard_ref[0]).astype(jnp.bfloat16)
    tile = dot(rows, dot(tile_ref[0], columns).astype(jnp.bfloat16))
    base_ref[0] = tile - dot(left, solved)
    row = lax.broadcasted_iota(jnp.int32, keep_ref.shape[1:], 0)
    column = lax.broadcasted_iota(jnp.int32, keep_ref.shape[1:], 1)
    length = length_ref[place]
    keep_ref[0] = jnp.where((row < length) & (column < length), 1.0, 0.0)

    @pl.when(place == 0)
    def _():
        row = lax.broadcasted_iota(jnp.int32, codes_ref.shape, 0)
        codes_ref[...] = jnp.where(row == 0, code_ref[0], code_ref[1]).astype(jnp.float32).astype(jnp.bfloat16)


def directions():
    odd = lax.rem(lax.axis_index("box"), 2)
    return 1 - odd, odd


def load_kernel(first, *refs):
    count = (len(refs) - 1) // 2
    sources, outs, sems = refs[:count], refs[count : 2 * count], refs[2 * count]
    copies = []
    for source, out in zip(sources, outs):
        for piece, target in pieces(first, source, out):
            copies.append(pltpu.make_async_copy(piece, target, sems.at[len(copies)]))
    for each in copies:
        each.start()
    for each in copies:
        each.wait()


def pieces(first, source, out):
    if len(source.shape) != 4:
        return [(source, out)]
    along = directions()
    return [
        (source.at[place, first + along[which]], out.at[2 * which + place])
        for which in range(2)
        for place in range(2)
    ]


def reduce_kernel(
    first, table_ref, inverse_ref, right_ref, left_ref, site, inverse, reduced, left, right, sems
):
    early, late = [], []
    for group, source, out in (
        (early, right_ref, right),
        (early, inverse_ref, inverse),
        (late, left_ref, left),
        (late, table_ref, site),
    ):
        for piece, target in pieces(first, source, out):
            group.append(pltpu.make_async_copy(piece, target, sems.at[len(early) + len(late)]))
    for each in early + late:
        each.start()
    for each in early:
        each.wait()
    for at in range(4):
        reduced[at] = dot(inverse[at % 2], right[at]).astype(jnp.bfloat16)
    for each in late:
        each.wait()


def targets_of(first, site_ref):
    along = directions()
    position = lax.axis_index("box")
    targets = []
    for which in range(2):
        there = position + offsets_list[first] * (1 - 2 * along[which])
        inside = (there >= 0) & (there < lax.axis_size("box"))
        row = []
        for place in range(2):
            one, two = (site_ref[place : place + 1, first + i : first + i + 1] for i in (which, 1 - which))
            row.append(jnp.where(inside, jnp.where(along[0] == 0, one, two), 2))
        targets.append(row)
    return targets


def join_places(targets, near):
    return [
        [sum(jnp.where(targets[w][p] == t, near[2 * w + p], 0.0) for p in range(2)) for t in range(2)]
        for w in range(2)
    ]


def whole_kernel(site_ref, inverse, right, left, out):
    reduced = [dot(inverse[at % 2], right[at]).astype(jnp.bfloat16) for at in range(4)]
    near = [dot(left[at], reduced[at]) for at in range(4)]
    sums = join_places(targets_of(0, site_ref), near)
    for which in range(2):
        for t in range(2):
            out[2 * which + t] = sums[which][t].astype(jnp.bfloat16)


def far_kernel(one_ref, two_ref, own_ref, site_ref, reduced, left, out_one, out_two):
    span = own_ref.shape[1]
    position = lax.axis_index("box")
    inner = lax.rem(lax.div(position + 1, 2), 2) == 1
    from_there = [jnp.where(inner, a[...], b[...]) for a, b in ((one_ref, two_ref), (two_ref, one_ref))]
    targets = targets_of(2, site_ref)
    picks = []
    for which in range(2):
        slots = from_there[which]
        for place in range(2):
            own_slots = jnp.where(targets[which][place] == 0, slots[0:1], slots[1:2])
            picks.append(pickers(own_slots, left.shape[1]))
    picked = [dot(reduced[at], picks[at][0]).astype(jnp.bfloat16) for at in range(4)]
    coupled = [dot(picks[at][1], left[at]).astype(jnp.bfloat16) for at in range(4)]
    near = [dot(coupled[at], picked[at]) for at in range(4)]
    updates = join_places(targets, near)
    own = own_ref[...]
    row = lax.broadcasted_iota(jnp.int32, (CODE_ROWS, span), 0)
    halves = (own >> 1, own & 1)
    code = jnp.zeros((CODE_ROWS, span), jnp.int32)
    for at in range(4):
        code = jnp.where(row == at, halves[at // 2][at % 2 : at % 2 + 1], code)
    code = code.astype(jnp.float32).astype(jnp.bfloat16)
    for out, update in zip((out_one, out_two), updates):
        for t in range(2):
            out[t * span : (t + 1) * span] = update[t].astype(jnp.bfloat16)
        out[2 * span :] = code


def step_kernel(one_ref, two_ref, near_ref, out_one, out_two):
    span = out_one.shape[1]
    passed = (one_ref, two_ref)
    picks = []
    for which in range(2):
        code = passed[which][2 * span :].astype(jnp.float32).astype(jnp.int32)
        slots = code[0:2] * 2 + code[2:4]
        picks += [pickers(slots[t : t + 1], near_ref.shape[1]) for t in range(2)]
    half = [dot(near_ref[at], picks[at][0]).astype(jnp.bfloat16) for at in range(4)]
    near = [dot(picks[at][1], half[at]) for at in range(4)]
    for which, out in enumerate((out_one, out_two)):
        for t in range(2):
            far = passed[1 - which][t * span : (t + 1) * span].astype(jnp.float32)
            out[t] = (near[2 * which + t] + far).astype(jnp.bfloat16)


def child_kernel(base_ref, keep_ref, codes_ref, one_ref, two_ref, *outs):
    places, span = base_ref.shape[:2]
    for place in range(places):
        value = base_ref[place] - one_ref[place].astype(jnp.float32) - two_ref[place].astype(jnp.float32)
        outs[place][0:span] = (value * keep_ref[place]).astype(jnp.bfloat16)
    outs[0][span:] = codes_ref[...]


def choose_kernel(*refs):
    sources, (mine_ref, other_ref) = refs[:-2], refs[-2:]
    children = (sources[: len(sources) // 2], sources[len(sources) // 2 :])
    span = mine_ref.shape[1]
    region = lax.axis_index("region")
    partner = region + 1 - 2 * lax.rem(region, 2)
    codes = [ref[span:].astype(jnp.float32) for ref in children[0]]
    for out_ref, owner in ((mine_ref, region), (other_ref, partner)):
        for slot in range(2):
            wanted = (owner * 2 + slot).astype(jnp.float32)
            value = None
            for place in range(2):
                for ref, code in zip(children[place], codes):
                    hit = jnp.where(code[place : place + 1] == wanted, 1.0, 0.0).astype(jnp.bfloat16)
                    term = ref[0:span] * hit
                    value = term if value is None else value + term
            out_ref[slot] = value


def join_kernel(a_ref, b_ref, out_ref):
    out_ref[...] = a_ref[...] + b_ref[...]


def local(
    kept_diagonal_tile,
    discard_reciprocal,
    discard_by_kept,
    kept_by_discard,
    adjacent_discard_to_kept,
    adjacent_kept_to_discard,
    adjacent_site_table,
    retained_slots,
    kept_list_length,
    ancestor_site_map,
):
    places, tile_span = retained_slots.shape
    wide, tall = kept_diagonal_tile.shape[1], discard_reciprocal.shape[1]
    params = pltpu.CompilerParams(vmem_limit_bytes=LIMIT)
    small = jax.ShapeDtypeStruct((places, tile_span, tile_span), jnp.bfloat16)

    def block(rows, columns):
        return pl.BlockSpec((1, rows, columns), lambda l: (l, 0, 0))

    own = (kept_list_length, ancestor_site_map, retained_slots, kept_diagonal_tile, discard_reciprocal, discard_by_kept, kept_by_discard)

    def self_update(*own):
        return pl.pallas_call(
            self_kernel,
            grid=(places,),
            in_specs=[SMEM, SMEM, VMEM, block(wide, wide), block(tall, tall), block(tall, wide), block(wide, tall)],
            out_specs=[block(tile_span, tile_span)] * 2 + [pl.BlockSpec((CODE_ROWS, tile_span), lambda l: (0, 0))],
            out_shape=[jax.ShapeDtypeStruct((places, tile_span, tile_span), jnp.float32)] * 2
            + [jax.ShapeDtypeStruct((CODE_ROWS, tile_span), jnp.bfloat16)],
            compiler_params=params,
            name="self_update",
        )(*own)

    def load(first, sources):
        shapes = [(4,) + v.shape[2:] if v.ndim == 4 else v.shape for v in sources]
        return pl.pallas_call(
            functools.partial(load_kernel, first),
            in_specs=[HBM] * len(sources),
            out_specs=[VMEM] * len(sources),
            out_shape=[pltpu.VMEM(shape, v.dtype) for shape, v in zip(shapes, sources)],
            scratch_shapes=[pltpu.SemaphoreType.DMA((8,))],
            compiler_params=params,
            name="load",
        )(*[pltpu.with_memory_space_constraint(v, pltpu.HBM) for v in sources])

    coupled = (adjacent_kept_to_discard, adjacent_discard_to_kept)
    outer_slots = swap(retained_slots, 2, 1)
    far_slots = [swap(retained_slots, 2, 0), outer_slots]
    far_sources = (adjacent_site_table, discard_reciprocal) + coupled
    rights, lefts = (4, tall, wide), (4, wide, tall)
    site, inverse, reduced, far_left = pl.pallas_call(
        functools.partial(reduce_kernel, 2),
        in_specs=[HBM] * 4,
        out_specs=[VMEM] * 4,
        out_shape=[
            pltpu.VMEM(adjacent_site_table.shape, jnp.int32),
            pltpu.VMEM(discard_reciprocal.shape, jnp.bfloat16),
            pltpu.VMEM(rights, jnp.bfloat16),
            pltpu.VMEM(lefts, jnp.bfloat16),
        ],
        scratch_shapes=[pltpu.VMEM(rights, jnp.bfloat16), pltpu.SemaphoreType.DMA((10,))],
        compiler_params=params,
        name="load_reduce",
    )(*[pltpu.with_memory_space_constraint(v, pltpu.HBM) for v in far_sources])
    message = jax.ShapeDtypeStruct((places * tile_span + CODE_ROWS, tile_span), jnp.bfloat16)
    far = pl.pallas_call(
        far_kernel,
        in_specs=[VMEM] * 6,
        out_specs=[VMEM] * 2,
        out_shape=[message] * 2,
        compiler_params=params,
        name="far_update",
    )(*far_slots, retained_slots, site, reduced, far_left)
    passed = [swap(value, 1, parity) for value, parity in zip(far, (1, 0))]
    coupled, own, far = lax.optimization_barrier((coupled, own, far))
    near_pair = load(0, coupled)
    whole = pl.pallas_call(
        whole_kernel,
        in_specs=[VMEM] * 4,
        out_specs=VMEM,
        out_shape=jax.ShapeDtypeStruct((4, wide, wide), jnp.bfloat16),
        compiler_params=params,
        name="whole_update",
    )(site, inverse, *near_pair)
    sent = pl.pallas_call(
        step_kernel,
        in_specs=[VMEM] * 3,
        out_specs=[VMEM] * 2,
        out_shape=[small, small],
        compiler_params=params,
        name="near_update",
    )(*passed, whole)
    arrived = [swap(sent[0], 1, 1), swap(sent[1], 1, 0)]
    base = self_update(*own)

    half = jax.ShapeDtypeStruct((tile_span, tile_span), jnp.bfloat16)
    coded = jax.ShapeDtypeStruct((tile_span + CODE_ROWS, tile_span), jnp.bfloat16)
    one, two = pl.pallas_call(
        child_kernel,
        in_specs=[VMEM] * 5,
        out_specs=[VMEM] * 2,
        out_shape=[coded, half],
        compiler_params=params,
        name="child",
    )(*base, *arrived)

    one_back, two_ahead = shift(one, "region", 2), shift(two, "region", -2)
    two_back, one_ahead = shift(two, "region", 2), shift(one, "region", -2)
    one_far, two_far = shift(one_back, "region", 2), shift(two_ahead, "region", -2)
    gathered = [one, one_back, one_ahead, one_far, two, two_back, two_ahead, two_far]
    mine, other = pl.pallas_call(
        choose_kernel,
        in_specs=[VMEM] * 8,
        out_specs=[VMEM, VMEM],
        out_shape=[small, small],
        compiler_params=params,
        name="choose",
    )(*gathered)
    partners = [(i, i ^ 1) for i in range(lax.axis_size("region"))]
    received = lax.ppermute(other, "region", partners)
    return pl.pallas_call(
        join_kernel,
        in_specs=[VMEM] * 2,
        out_specs=VMEM,
        out_shape=small,
        compiler_params=params,
        name="join",
    )(mine, received)


def solution(mesh):
    in_specs = (
        P(("region", "box"), None, None),
        P(("region", "box"), None, None),
        P(("region", "box"), None, None),
        P(("region", "box"), None, None),
        P(("region", "box"), None, None, None),
        P(("region", "box"), None, None, None),
        P(("region", "box"), None),
        P(("region", "box"), None),
        P(("region", "box")),
        P(("region", "box")),
    )
    out_specs = P(("region", "box"), None, None)
    return jax.shard_map(local, mesh=mesh, in_specs=in_specs, out_specs=out_specs, check_vma=False)
```

```python
import functools

import jax
import jax.numpy as jnp
from jax import lax
from jax.experimental import pallas as pl
from jax.experimental.pallas import tpu as pltpu
from jax.sharding import PartitionSpec as P

offsets_list = (1, -1, 2, -2)
CODE_ROWS = 16
VMEM = pl.BlockSpec(memory_space=pltpu.VMEM)
HBM = pl.BlockSpec(memory_space=pltpu.HBM)
SMEM = pl.BlockSpec(memory_space=pltpu.SMEM)
LIMIT = 16 * 1024 * 1024
NEAR_LIMIT = 16 * 1024 * 1024


def shift(value, axis, by):
    length = lax.axis_size(axis)
    return lax.ppermute(value, axis, [(i, (i + by) % length) for i in range(length)])


def swap(value, by, parity):
    regions, length = lax.axis_size("region"), lax.axis_size("box")
    pairs = []
    for r in range(regions):
        for j in range(length):
            there = j + by if j // by % 2 == (parity + r) % 2 else j - by
            goal = (r, there) if 0 <= there < length else (r ^ 2, j)
            pairs.append((r * length + j, goal[0] * length + goal[1]))
    return lax.ppermute(value, ("region", "box"), pairs)


def dot(a, b):
    return jnp.dot(a, b, preferred_element_type=jnp.float32)


def pickers(slots, span):
    count = slots.shape[1]
    column = lax.broadcasted_iota(jnp.int32, (span, count), 0) == slots
    tall = jnp.broadcast_to(slots, (128, count)).T
    lane = lax.broadcasted_iota(jnp.int32, (count, 128), 1)
    row = [tall == lane + at for at in range(0, span, 128)]
    one, zero = jnp.float32(1.0), jnp.float32(0.0)
    columns = jnp.where(column, one, zero).astype(jnp.bfloat16)
    rows = jnp.concatenate([jnp.where(r, one, zero).astype(jnp.bfloat16) for r in row], axis=1)
    return columns, rows


def self_kernel(
    length_ref, code_ref, slots_ref, tile_ref, inverse_ref, by_kept_ref, by_discard_ref, base_ref, keep_ref, codes_ref
):
    place = pl.program_id(0)
    slots = jnp.where(place == 0, slots_ref[0:1, :], slots_ref[1:2, :])
    columns, rows = pickers(slots, tile_ref.shape[1])
    picked = dot(by_kept_ref[0], columns).astype(jnp.bfloat16)
    solved = dot(inverse_ref[0], picked).astype(jnp.bfloat16)
    left = dot(rows, by_discard_ref[0]).astype(jnp.bfloat16)
    tile = dot(rows, dot(tile_ref[0], columns).astype(jnp.bfloat16))
    base_ref[0] = tile - dot(left, solved)
    row = lax.broadcasted_iota(jnp.int32, keep_ref.shape[1:], 0)
    column = lax.broadcasted_iota(jnp.int32, keep_ref.shape[1:], 1)
    length = length_ref[place]
    keep_ref[0] = jnp.where((row < length) & (column < length), 1.0, 0.0)

    @pl.when(place == 0)
    def _():
        row = lax.broadcasted_iota(jnp.int32, codes_ref.shape, 0)
        codes_ref[...] = jnp.where(row == 0, code_ref[0], code_ref[1]).astype(jnp.float32).astype(jnp.bfloat16)


def directions():
    odd = lax.rem(lax.axis_index("box") + lax.axis_index("region"), 2)
    return 1 - odd, odd


def load_kernel(first, *refs):
    count = (len(refs) - 1) // 2
    sources, outs, sems = refs[:count], refs[count : 2 * count], refs[2 * count]
    copies = []
    for source, out in zip(sources, outs):
        for piece, target in pieces(first, source, out):
            copies.append(pltpu.make_async_copy(piece, target, sems.at[len(copies)]))
    for each in copies:
        each.start()
    for each in copies:
        each.wait()


def pieces(first, source, out):
    if len(source.shape) != 4:
        return [(source, out)]
    along = directions()
    return [
        (source.at[place, first + along[which]], out.at[2 * which + place])
        for which in range(2)
        for place in range(2)
    ]


def reduce_kernel(
    first, table_ref, inverse_ref, right_ref, left_ref, site, inverse, reduced, left, right, sems
):
    early, late = [], []
    for group, source, out in (
        (early, right_ref, right),
        (early, inverse_ref, inverse),
        (late, left_ref, left),
        (late, table_ref, site),
    ):
        for piece, target in pieces(first, source, out):
            group.append(pltpu.make_async_copy(piece, target, sems.at[len(early) + len(late)]))
    for each in early + late:
        each.start()
    for each in early:
        each.wait()
    for at in range(4):
        reduced[at] = dot(inverse[at % 2], right[at]).astype(jnp.bfloat16)
    for each in late:
        each.wait()


def targets_of(first, site_ref):
    along = directions()
    position = lax.axis_index("box")
    targets = []
    for which in range(2):
        there = position + offsets_list[first] * (1 - 2 * along[which])
        inside = (there >= 0) & (there < lax.axis_size("box"))
        row = []
        for place in range(2):
            one, two = (site_ref[place : place + 1, first + i : first + i + 1] for i in (which, 1 - which))
            row.append(jnp.where(inside, jnp.where(along[0] == 0, one, two), 2))
        targets.append(row)
    return targets


def join_places(targets, near):
    return [
        [sum(jnp.where(targets[w][p] == t, near[2 * w + p], 0.0) for p in range(2)) for t in range(2)]
        for w in range(2)
    ]


def whole_kernel(site_ref, inverse, right, left, out):
    reduced = [dot(inverse[at % 2], right[at]).astype(jnp.bfloat16) for at in range(4)]
    near = [dot(left[at], reduced[at]) for at in range(4)]
    sums = join_places(targets_of(0, site_ref), near)
    for which in range(2):
        for t in range(2):
            out[2 * which + t] = sums[which][t].astype(jnp.bfloat16)


def far_kernel(one_ref, two_ref, own_ref, site_ref, reduced, left, out_one, out_two):
    span = own_ref.shape[1]
    position = lax.axis_index("box")
    inner = lax.rem(lax.div(position + 1, 2), 2) == 1
    from_there = [jnp.where(inner, a[...], b[...]) for a, b in ((one_ref, two_ref), (two_ref, one_ref))]
    targets = targets_of(2, site_ref)
    picks = []
    for which in range(2):
        slots = from_there[which]
        for place in range(2):
            own_slots = jnp.where(targets[which][place] == 0, slots[0:1], slots[1:2])
            picks.append(pickers(own_slots, left.shape[1]))
    picked = [dot(reduced[at], picks[at][0]).astype(jnp.bfloat16) for at in range(4)]
    coupled = [dot(picks[at][1], left[at]).astype(jnp.bfloat16) for at in range(4)]
    near = [dot(coupled[at], picked[at]) for at in range(4)]
    updates = join_places(targets, near)
    own = own_ref[...]
    row = lax.broadcasted_iota(jnp.int32, (CODE_ROWS, span), 0)
    halves = (own >> 1, own & 1)
    code = jnp.zeros((CODE_ROWS, span), jnp.int32)
    for at in range(4):
        code = jnp.where(row == at, halves[at // 2][at % 2 : at % 2 + 1], code)
    code = code.astype(jnp.float32).astype(jnp.bfloat16)
    for out, update in zip((out_one, out_two), updates):
        for t in range(2):
            out[t * span : (t + 1) * span] = update[t].astype(jnp.bfloat16)
        out[2 * span :] = code


def step_kernel(one_ref, two_ref, near_ref, out_one, out_two):
    span = out_one.shape[1]
    passed = (one_ref, two_ref)
    picks = []
    for which in range(2):
        code = passed[which][2 * span :].astype(jnp.float32).astype(jnp.int32)
        slots = code[0:2] * 2 + code[2:4]
        picks += [pickers(slots[t : t + 1], near_ref.shape[1]) for t in range(2)]
    half = [dot(near_ref[at], picks[at][0]).astype(jnp.bfloat16) for at in range(4)]
    near = [dot(picks[at][1], half[at]) for at in range(4)]
    for which, out in enumerate((out_one, out_two)):
        for t in range(2):
            far = passed[1 - which][t * span : (t + 1) * span].astype(jnp.float32)
            out[t] = (near[2 * which + t] + far).astype(jnp.bfloat16)


def child_kernel(base_ref, keep_ref, codes_ref, one_ref, two_ref, *outs):
    places, span = base_ref.shape[:2]
    for place in range(places):
        value = base_ref[place] - one_ref[place].astype(jnp.float32) - two_ref[place].astype(jnp.float32)
        outs[place][0:span] = (value * keep_ref[place]).astype(jnp.bfloat16)
    outs[0][span:] = codes_ref[...]


def choose_kernel(*refs):
    sources, (mine_ref, other_ref) = refs[:-2], refs[-2:]
    children = (sources[: len(sources) // 2], sources[len(sources) // 2 :])
    span = mine_ref.shape[1]
    region = lax.axis_index("region")
    partner = region + 1 - 2 * lax.rem(region, 2)
    codes = [ref[span:].astype(jnp.float32) for ref in children[0]]
    for out_ref, owner in ((mine_ref, region), (other_ref, partner)):
        for slot in range(2):
            wanted = (owner * 2 + slot).astype(jnp.float32)
            value = None
            for place in range(2):
                for ref, code in zip(children[place], codes):
                    hit = jnp.where(code[place : place + 1] == wanted, 1.0, 0.0).astype(jnp.bfloat16)
                    term = ref[0:span] * hit
                    value = term if value is None else value + term
            out_ref[slot] = value


def join_kernel(a_ref, b_ref, out_ref):
    out_ref[...] = a_ref[...] + b_ref[...]


def local(
    kept_diagonal_tile,
    discard_reciprocal,
    discard_by_kept,
    kept_by_discard,
    adjacent_discard_to_kept,
    adjacent_kept_to_discard,
    adjacent_site_table,
    retained_slots,
    kept_list_length,
    ancestor_site_map,
):
    places, tile_span = retained_slots.shape
    wide, tall = kept_diagonal_tile.shape[1], discard_reciprocal.shape[1]
    params = pltpu.CompilerParams(vmem_limit_bytes=LIMIT)
    small = jax.ShapeDtypeStruct((places, tile_span, tile_span), jnp.bfloat16)

    def block(rows, columns):
        return pl.BlockSpec((1, rows, columns), lambda l: (l, 0, 0))

    own = (kept_list_length, ancestor_site_map, retained_slots, kept_diagonal_tile, discard_reciprocal, discard_by_kept, kept_by_discard)

    def self_update(*own):
        return pl.pallas_call(
            self_kernel,
            grid=(places,),
            in_specs=[SMEM, SMEM, VMEM, block(wide, wide), block(tall, tall), block(tall, wide), block(wide, tall)],
            out_specs=[block(tile_span, tile_span)] * 2 + [pl.BlockSpec((CODE_ROWS, tile_span), lambda l: (0, 0))],
            out_shape=[jax.ShapeDtypeStruct((places, tile_span, tile_span), jnp.float32)] * 2
            + [jax.ShapeDtypeStruct((CODE_ROWS, tile_span), jnp.bfloat16)],
            compiler_params=params,
            name="self_update",
        )(*own)

    def load(first, sources):
        shapes = [(4,) + v.shape[2:] if v.ndim == 4 else v.shape for v in sources]
        return pl.pallas_call(
            functools.partial(load_kernel, first),
            in_specs=[HBM] * len(sources),
            out_specs=[VMEM] * len(sources),
            out_shape=[pltpu.VMEM(shape, v.dtype) for shape, v in zip(shapes, sources)],
            scratch_shapes=[pltpu.SemaphoreType.DMA((8,))],
            compiler_params=params,
            name="load",
        )(*[pltpu.with_memory_space_constraint(v, pltpu.HBM) for v in sources])

    coupled = (adjacent_kept_to_discard, adjacent_discard_to_kept)
    outer_slots = swap(retained_slots, 2, 1)
    far_slots = [swap(retained_slots, 2, 0), outer_slots]
    far_sources = (adjacent_site_table, discard_reciprocal) + coupled
    rights, lefts = (4, tall, wide), (4, wide, tall)
    site, inverse, reduced, far_left = pl.pallas_call(
        functools.partial(reduce_kernel, 2),
        in_specs=[HBM] * 4,
        out_specs=[VMEM] * 4,
        out_shape=[
            pltpu.VMEM(adjacent_site_table.shape, jnp.int32),
            pltpu.VMEM(discard_reciprocal.shape, jnp.bfloat16),
            pltpu.VMEM(rights, jnp.bfloat16),
            pltpu.VMEM(lefts, jnp.bfloat16),
        ],
        scratch_shapes=[pltpu.VMEM(rights, jnp.bfloat16), pltpu.SemaphoreType.DMA((10,))],
        compiler_params=params,
        name="load_reduce",
    )(*[pltpu.with_memory_space_constraint(v, pltpu.HBM) for v in far_sources])
    message = jax.ShapeDtypeStruct((places * tile_span + CODE_ROWS, tile_span), jnp.bfloat16)
    far = pl.pallas_call(
        far_kernel,
        in_specs=[VMEM] * 6,
        out_specs=[VMEM] * 2,
        out_shape=[message] * 2,
        compiler_params=params,
        name="far_update",
    )(*far_slots, retained_slots, site, reduced, far_left)
    passed = [swap(value, 1, parity) for value, parity in zip(far, (1, 0))]
    coupled, own, far = lax.optimization_barrier((coupled, own, far))
    near_pair = load(0, coupled)
    whole = pl.pallas_call(
        whole_kernel,
        in_specs=[VMEM] * 4,
        out_specs=VMEM,
        out_shape=jax.ShapeDtypeStruct((4, wide, wide), jnp.bfloat16),
        compiler_params=params,
        name="whole_update",
    )(site, inverse, *near_pair)
    sent = pl.pallas_call(
        step_kernel,
        in_specs=[VMEM] * 3,
        out_specs=[VMEM] * 2,
        out_shape=[small, small],
        compiler_params=params,
        name="near_update",
    )(*passed, whole)
    arrived = [swap(sent[0], 1, 1), swap(sent[1], 1, 0)]
    base = self_update(*own)

    half = jax.ShapeDtypeStruct((tile_span, tile_span), jnp.bfloat16)
    coded = jax.ShapeDtypeStruct((tile_span + CODE_ROWS, tile_span), jnp.bfloat16)
    one, two = pl.pallas_call(
        child_kernel,
        in_specs=[VMEM] * 5,
        out_specs=[VMEM] * 2,
        out_shape=[coded, half],
        compiler_params=params,
        name="child",
    )(*base, *arrived)

    one_back, two_ahead = shift(one, "region", 2), shift(two, "region", -2)
    two_back, one_ahead = shift(two, "region", 2), shift(one, "region", -2)
    one_far, two_far = shift(one_back, "region", 2), shift(two_ahead, "region", -2)
    gathered = [one, one_back, one_ahead, one_far, two, two_back, two_ahead, two_far]
    mine, other = pl.pallas_call(
        choose_kernel,
        in_specs=[VMEM] * 8,
        out_specs=[VMEM, VMEM],
        out_shape=[small, small],
        compiler_params=params,
        name="choose",
    )(*gathered)
    partners = [(i, i ^ 1) for i in range(lax.axis_size("region"))]
    received = lax.ppermute(other, "region", partners)
    return pl.pallas_call(
        join_kernel,
        in_specs=[VMEM] * 2,
        out_specs=VMEM,
        out_shape=small,
        compiler_params=params,
        name="join",
    )(mine, received)


def solution(mesh):
    in_specs = (
        P(("region", "box"), None, None),
        P(("region", "box"), None, None),
        P(("region", "box"), None, None),
        P(("region", "box"), None, None),
        P(("region", "box"), None, None, None),
        P(("region", "box"), None, None, None),
        P(("region", "box"), None),
        P(("region", "box"), None),
        P(("region", "box")),
        P(("region", "box")),
    )
    out_specs = P(("region", "box"), None, None)
    return jax.shard_map(local, mesh=mesh, in_specs=in_specs, out_specs=out_specs, check_vma=False)
```
